256 devices in a mesh: rep: 32 (over y, x, core), fsdp: 8 (over z).
Axes of the slice: x: 4, y: 4, z: 8, core: 2. Of those that a mesh axis runs over, the one named last changes fastest.
Arguments:
- codes: bfloat16 [32, 4096, 1024], P('rep', 'fsdp'), may hold values from -127 to 127
- block_scales: float32 [32, 4096, 8], P('rep', 'fsdp'), may hold values from 0.002 to 0.02
- params: bfloat16 [4096, 1024], P('fsdp'), may hold values from -6 to 6
- momentum: bfloat16 [4096, 1024], P('fsdp'), may hold values from -3 to 3
Outputs:
- new_params: bfloat16 [4096, 1024], replicated
- new_momentum: bfloat16 [4096, 1024], P('fsdp')
The draws below stay inside these ranges and needn't reach their ends.
All inputs are finite; a program needn't handle non-finite values.
Results may differ from the reference program's by a relative error of at most 0.006.
Values may be sent and summed in bfloat16 or wider, within the bound.
A program may use at most 64 MiB of HBM per device.

```python
import math
import jax
import jax.numpy as jnp
from jax import lax

D = 4096
KV = 1024
BLOCK = 128
REP = 32
N_REP = 32


def levels(rng, extent, shards, low, top_value):
    level, own = 1.0, jax.random.fold_in(rng, 6)
    for dim, shards_of in shards:
        steps = jnp.exp(jax.random.uniform(jax.random.fold_in(own, dim), (shards_of,), jnp.float32, low / len(shards), top_value / len(shards)))
        level = level * jnp.repeat(steps, extent[dim] // shards_of).reshape([-1 if axis == dim else 1 for axis in range(len(extent))])
    return level


def centred(key, extent, scale, limit, split=(), dtype=jnp.bfloat16):
    array = jax.random.normal(key, extent, jnp.float32) * scale
    if len(split) > 0:
        array = levels(key, extent, split, -0.22, 0.18) * array
    return jnp.clip(array, min=-limit, max=limit).astype(dtype)


def setup_inputs(seed: int = 0) -> dict:
    key_of = jax.random.split(jax.random.key(seed), 5)
    return {
        "codes": centred(key_of[0], (REP, D, KV), 40.0, 127.0, ((0, 32), (1, 8))),
        "block_scales": jnp.clip(jnp.exp(math.log(0.02) - 2.30258502 * jax.random.uniform(key_of[1], (REP, D, KV // BLOCK), jnp.float32) ** levels(key_of[1], (REP, D, KV // BLOCK), ((0, 32), (1, 8)), -0.2, 0.2)), 0.002, 0.02),
        "params": centred(key_of[2], (D, KV), 1.0, 6.0, ((0, 8),)),
        "momentum": centred(key_of[3], (D, KV), 0.5, 3.0, ((0, 8),)),
    }


def reference(codes, block_scales, params, momentum):
    def accumulate(total, pair):
        code_block, scale_block = pair
        pieces = code_block.astype(jnp.float32).reshape(D, KV // BLOCK, BLOCK) * scale_block[:, :, None]
        return total + pieces.reshape(D, KV), None

    total, unused = lax.scan(accumulate, jnp.zeros((D, KV), jnp.float32), (codes, block_scales))
    delta = total / N_REP
    moment = 0.9 * momentum.astype(jnp.float32) + delta
    new_params = (params.astype(jnp.float32) - 0.7 * (delta + 0.9 * moment)).astype(jnp.bfloat16)
    return new_params, moment.astype(jnp.bfloat16)
```

```python
import functools

import jax
import jax.numpy as jnp
from jax import lax
from jax.experimental import pallas as pl
from jax.experimental.pallas import tpu as pltpu
from jax.sharding import PartitionSpec as P

MESH = pl.DeviceIdType.MESH
NX, NY, NZ = 4, 4, 8
ROWS, COLS, BLOCK = 512, 1024, 128
HALF = ROWS // 2
PIECE = 16
NEAR = (0, 1, -1, 2, -2, 3, -3, 4)
PLACE = {d: i for i, d in enumerate(NEAR)} | {-4: 7}
A, B, C = (0, 384), (384, 384), (768, 256)
AB = 768
WAVES = ((0, 1), (1, 2), (3, 2), (5, 3))
PLANE = [(dx, dy) for dy in (0, 1, -1, 2) for dx in (0, 1, -1, 2) if (dx, dy) != (0, 0)]
COPIES = 160


def position():
    r, z = lax.axis_index("rep"), lax.axis_index("fsdp")
    return lax.rem(lax.div(r, 2), NX), lax.div(r, 2 * NX), z, lax.rem(r, 2)


def step_of(delta, params, momentum):
    delta = delta.astype(jnp.float32)
    moment = 0.9 * momentum.astype(jnp.float32) + delta
    updated = params.astype(jnp.float32) - 0.7 * (delta + 0.9 * moment)
    return updated.astype(jnp.bfloat16), moment.astype(jnp.bfloat16)


def exchange(codes, scales, params, momentum, full, own_params, own_moment,
             codes_v, scales_v, params_v, momentum_v, sib_out, sib_in, chip_sum, arrived, piece, ring,
             load_sem, send_sem, recv_sem):
    x, y, z, c = position()
    other = 1 - c

    def device(dx=0, dy=0, dz=0, dc=0):
        rep = (lax.rem(y + dy + NY, NY) * NX + lax.rem(x + dx + NX, NX)) * 2 + (other if dc else c)
        return rep, lax.rem(z + dz + NZ, NZ)

    loads = [pltpu.make_async_copy(src, dst, load_sem.at[i]) for i, (src, dst) in enumerate(
        ((codes, codes_v), (scales, scales_v), (params, params_v), (momentum, momentum_v)))]
    for load in loads:
        load.start()

    barrier = pltpu.get_barrier_semaphore()
    partners = [dict(dc=1)] + [dict(dx=dx, dy=dy) for dx, dy in PLANE] + [dict(dz=dz) for dz in NEAR[1:]]
    for partner in partners:
        pl.semaphore_signal(barrier, inc=1, device_id=device(**partner), device_id_type=MESH)

    sent = []

    def send(src, dst, **to):
        i = len(sent)
        copy = pltpu.make_async_remote_copy(src, dst, send_sem.at[i], recv_sem.at[i],
                                            device_id=device(**to), device_id_type=MESH)
        copy.start()
        sent.append(copy)
        return copy

    def got(*copies):
        for copy in copies:
            copy.wait_recv()

    def dequantized(half, chunk, block):
        start = pl.multiple_of(half * HALF + chunk * 128, 128)
        turned = scales_v[:, pl.ds(start, 128)].T
        codes_f = codes_v[pl.ds(start, 128), block * BLOCK:(block + 1) * BLOCK].astype(jnp.float32)
        return codes_f * turned[:, block:block + 1]

    loads[0].wait()
    loads[1].wait()
    halves = []
    for chunk in range(2):
        rows = slice(chunk * 128, (chunk + 1) * 128)
        for block in range(8):
            sib_out[rows, block * BLOCK:(block + 1) * BLOCK] = dequantized(other, chunk, block).astype(jnp.bfloat16)
        if chunk == 0:
            pl.semaphore_wait(barrier, len(partners))
        halves.append(send(sib_out.at[rows], sib_in.at[rows], dc=1))
    for chunk in range(2):
        rows = slice(chunk * 128, (chunk + 1) * 128)
        got(halves[chunk])
        for block in range(8):
            cols = slice(block * BLOCK, (block + 1) * BLOCK)
            total = dequantized(c, chunk, block) + sib_in[rows, cols].astype(jnp.float32)
            chip_sum[2 * chunk:2 * chunk + 2, :, :, cols] = total.astype(jnp.bfloat16).reshape(2, NX, PIECE, BLOCK)

    pieces = []
    for i, (dx, dy) in enumerate(PLANE):
        theirs = chip_sum.at[lax.rem(y + dy + NY, NY), lax.rem(x + dx + NX, NX)]
        pieces.append(send(theirs, arrived.at[i], dx=dx, dy=dy))
    loads[2].wait()
    loads[3].wait()
    total = chip_sum[y, x].astype(jnp.float32)
    for i, copy in enumerate(pieces):
        got(copy)
        total = total + arrived[i].astype(jnp.float32)
    delta = (total / 32).astype(jnp.bfloat16)
    start = pl.multiple_of(c * HALF + y * 64 + x * PIECE, PIECE)
    full[0, c, y, x] = delta
    piece[...] = step_of(delta, params_v[pl.ds(start, PIECE)], momentum_v[pl.ds(start, PIECE)])[0]

    def at(place, count, rows_y, rows_x, group):
        return full.at[pl.ds(place, count), c, rows_y, rows_x, :, pl.ds(*group)]

    def second(wave, group):
        block = at(*WAVES[wave], y, x, group)
        return [send(block, block, **{"dx" if group is A else "dy": d}) for d in (1, -1, 2)]

    def halves_of(wave, group, back):
        for i in range(2):
            if group is A:
                yield at(*WAVES[wave], lax.rem(y - back + NY, NY), pl.ds(2 * i, 2), group)
            else:
                yield at(*WAVES[wave], pl.ds(2 * i, 2), lax.rem(x - back + NX, NX), group)

    def third(wave, group):
        axis = "dy" if group is A else "dx"
        one, two = halves_of(wave, group, 0)
        return (send(one, one, **{axis: 1}), send(two, two, **{axis: -1}),
                send(two, two, **{axis: 1}), send(one, one, **{axis: -1}))

    def onward(wave, group, copies):
        axis = "dy" if group is A else "dx"
        one, _ = halves_of(wave, group, 1)
        _, two = halves_of(wave, group, -1)
        got(copies[0])
        ahead = send(one, one, **{axis: 1})
        got(copies[1])
        return (*copies[2:], ahead, send(two, two, **{axis: -1}))

    def to_sibling(place, count, group):
        block = full.at[pl.ds(place, count), c, :, :, :, pl.ds(*group)]
        return send(block, block, dc=1)

    S2, S3, S4, handed = {}, {}, {}, []

    for group in (A, B):
        S2[0, group] = second(0, group)
    plane_c = []
    block = full.at[0, c, y, x, :, pl.ds(*C)]
    for dx, dy in PLANE:
        plane_c.append(send(block, block, dx=dx, dy=dy))
    along = {}
    for dz in NEAR[1:]:
        place = PLACE[-dz]
        along[place] = send(piece.at[:, pl.ds(0, AB)], full.at[place, c, y, x, :, pl.ds(0, AB)], dz=dz)

    def start_second(wave):
        first, count = WAVES[wave]
        got(*(along[i] for i in range(first, first + count)))
        for group in (A, B):
            S2[wave, group] = second(wave, group)

    def start_third(wave):
        for group in (A, B):
            got(*S2[wave, group])
            S3[wave, group] = third(wave, group)

    def start_onward(wave):
        for group in (A, B):
            S4[wave, group] = onward(wave, group, S3[wave, group])

    def finish(wave):
        for group in (A, B):
            got(*S4[wave, group])
            handed.append(to_sibling(*WAVES[wave], group))

    def ring_at(d, rows=slice(None)):
        return full.at[PLACE[d], c, rows, :, :, pl.ds(*C)]

    up, down = {}, {}

    def ring_step(n):
        got(up[n])
        got(down[n])
        if n < 3:
            up[n + 1] = send(ring_at(-n), ring_at(-n - 1), dz=1)
            down[n + 1] = send(ring_at(n), ring_at(n + 1), dz=-1)
        elif n == 3:
            up[4] = send(ring_at(-3, pl.ds(0, 2)), ring_at(4, pl.ds(0, 2)), dz=1)
            down[4] = send(ring_at(3, pl.ds(2, 2)), ring_at(4, pl.ds(2, 2)), dz=-1)
        if n < 4:
            handed.append(to_sibling(PLACE[n], 2, C))
        else:
            handed.append(to_sibling(PLACE[4], 1, C))

    start_third(0)
    start_second(1)
    got(*plane_c)
    for row in range(NY):
        start = pl.multiple_of(c * HALF + row * 64, 64)
        moved = full[0, c, row, :, :, C[0]:C[0] + C[1]].reshape(64, C[1])
        cols = slice(C[0], C[0] + C[1])
        ring[row] = step_of(moved, params_v[pl.ds(start, 64), cols], momentum_v[pl.ds(start, 64), cols])[0].reshape(
            NX, PIECE, C[1])
    up[1] = send(ring, ring_at(-1), dz=1)
    down[1] = send(ring, ring_at(1), dz=-1)
    handed.append(to_sibling(0, 1, C))
    start_second(2)
    start_onward(0)
    start_third(1)
    start_second(3)
    finish(0)
    ring_step(1)
    start_third(2)
    start_onward(1)
    start_third(3)
    ring_step(2)
    finish(1)

    got(*handed[:3])
    del handed[:3]
    for i in range(2):
        for row in range(NY):
            start = i * HALF + row * 64
            moved = full[0, i, row].reshape(64, COLS)
            updated, moment = step_of(moved, params_v[start:start + 64], momentum_v[start:start + 64])
            own_params[start:start + 64] = updated
            own_moment[start:start + 64] = moment

    start_onward(2)
    ring_step(3)
    finish(2)
    start_onward(3)
    finish(3)
    ring_step(4)
    got(*handed)
    for copy in sent:
        copy.wait_send()


def write_out(full, own_params, own_moment, new_params, new_momentum, sem):
    z = lax.axis_index("fsdp")
    copies = []
    for i, d in enumerate(NEAR[1:], 1):
        copies.append(pltpu.make_async_copy(full.at[i], new_params.at[lax.rem(z + d + NZ, NZ)], sem.at[i]))
    copies.append(pltpu.make_async_copy(own_params, new_params.at[z], sem.at[0]))
    copies.append(pltpu.make_async_copy(own_moment, new_momentum, sem.at[8]))
    for copy in copies:
        copy.start()
    for copy in copies:
        copy.wait()


def local(codes, block_scales, params, momentum):
    bf16 = jnp.bfloat16
    slab = (2, NY, NX, PIECE, COLS)
    hbm, vmem = pl.BlockSpec(memory_space=pltpu.HBM), pl.BlockSpec(memory_space=pltpu.VMEM)
    full, own_params, own_moment = pl.pallas_call(
        exchange,
        name="exchange",
        out_shape=(pltpu.VMEM((NZ, *slab), bf16), pltpu.VMEM((ROWS, COLS), bf16), pltpu.VMEM((ROWS, COLS), bf16)),
        in_specs=[hbm] * 4,
        out_specs=[vmem] * 3,
        scratch_shapes=[
            pltpu.VMEM((ROWS, COLS), bf16),
            pltpu.VMEM((COLS // BLOCK, ROWS), jnp.float32),
            pltpu.VMEM((ROWS, COLS), bf16),
            pltpu.VMEM((ROWS, COLS), bf16),
            pltpu.VMEM((HALF, COLS), bf16),
            pltpu.VMEM((HALF, COLS), bf16),
            pltpu.VMEM((NY, NX, PIECE, COLS), bf16),
            pltpu.VMEM((len(PLANE), PIECE, COLS), bf16),
            pltpu.VMEM((PIECE, COLS), bf16),
            pltpu.VMEM((NY, NX, PIECE, C[1]), bf16),
            pltpu.SemaphoreType.DMA((4,)),
            pltpu.SemaphoreType.DMA((COPIES,)),
            pltpu.SemaphoreType.DMA((COPIES,)),
        ],
        compiler_params=pltpu.CompilerParams(
            collective_id=0, has_side_effects=True, vmem_limit_bytes=32 * 2**20
        ),
    )(codes[0], block_scales[0].T, params, momentum)
    new_params, new_momentum = pl.pallas_call(
        write_out,
        name="write_out",
        out_shape=(jax.ShapeDtypeStruct((NZ, *slab), bf16), jax.ShapeDtypeStruct((ROWS, COLS), bf16)),
        in_specs=[vmem] * 3,
        out_specs=[hbm] * 2,
        scratch_shapes=[pltpu.SemaphoreType.DMA((9,))],
        compiler_params=pltpu.CompilerParams(vmem_limit_bytes=32 * 2**20),
    )(full, own_params.reshape(slab), own_moment)
    return new_params.reshape(NZ * ROWS, COLS), new_momentum


def solution(mesh):
    return jax.shard_map(
        local, mesh=mesh, in_specs=(P("rep", "fsdp", None), P("rep", "fsdp", None), P("fsdp", None), P("fsdp", None)),
        out_specs=(P(), P("fsdp", None)), check_vma=False
    )
```

```python
import functools

import jax
import jax.numpy as jnp
from jax import lax
from jax.experimental import pallas as pl
from jax.experimental.pallas import tpu as pltpu
from jax.sharding import PartitionSpec as P

MESH = pl.DeviceIdType.MESH
NX, NY, NZ = 4, 4, 8
ROWS, COLS, BLOCK = 512, 1024, 128
HALF = ROWS // 2
PIECE = 16
NEAR = (0, 1, -1, 2, -2, 3, -3, 4)
PLACE = {d: i for i, d in enumerate(NEAR)} | {-4: 7}
AB = 640
C = (AB, COLS - AB)
WAVES = ((0, 1, 384), (1, 2, 256), (3, 2, 256), (5, 3, 384))
SPLIT = {C: ((640, 128), (768, 256)), (0, AB): ((0, 384), (384, 256))}
LINE = (1, -1, 2)
PLANE = [(dx, dy) for dy in (0, 1, -1, 2) for dx in (0, 1, -1, 2) if (dx, dy) != (0, 0)]
GROUPS = ("A", "B")
COPIES = 160
ORDER = (
    ("line_c",), ("line_ab",), ("sum_c",), ("sum_ab",), ("second", 1), ("ring_start",), ("third", 0), ("second", 2), ("second", 3),
    ("third", 1), ("onward", 0), ("ring", 1), ("third", 2), ("onward", 1), ("third", 3), ("finish", 0),
    ("ring", 2), ("onward", 2), ("finish", 1), ("own",), ("onward", 3), ("finish", 2), ("ring", 3), ("finish", 3), ("ring", 4),
)


def position():
    r, z = lax.axis_index("rep"), lax.axis_index("fsdp")
    return lax.rem(lax.div(r, 2), NX), lax.div(r, 2 * NX), z, lax.rem(r, 2)


def step_of(delta, params, momentum):
    delta = delta.astype(jnp.float32)
    moment = 0.9 * momentum.astype(jnp.float32) + delta
    updated = params.astype(jnp.float32) - 0.7 * (delta + 0.9 * moment)
    return updated.astype(jnp.bfloat16), moment.astype(jnp.bfloat16)


def exchange(codes, scales, params, momentum, full, own_params, own_moment,
             codes_v, scales_v, params_v, momentum_v, sib_out, sib_in, chip_sum, line_in, line_sum, last_in, piece, ring,
             load_sem, send_sem, recv_sem):
    x, y, z, c = position()
    other = 1 - c

    known = {}

    def device(dx=0, dy=0, dz=0, dc=0):
        to = (dx % NX, dy % NY, dz % NZ, dc)
        if to not in known:
            across = lax.rem(x + to[0], NX) if to[0] else x
            along_y = lax.rem(y + to[1], NY) if to[1] else y
            known[to] = (along_y * NX + across) * 2 + (other if dc else c), lax.rem(z + to[2], NZ) if to[2] else z
        return known[to]

    loads = [pltpu.make_async_copy(src, dst, load_sem.at[i]) for i, (src, dst) in enumerate(
        ((codes, codes_v), (scales, scales_v), (params, params_v), (momentum, momentum_v)))]
    for load in loads:
        load.start()

    barrier = pltpu.get_barrier_semaphore()
    partners = [dict(dc=1)] + [dict(dx=dx, dy=dy) for dx, dy in PLANE] + [dict(dz=dz) for dz in NEAR[1:]]
    for partner in partners:
        pl.semaphore_signal(barrier, inc=1, device_id=device(**partner), device_id_type=MESH)

    sent = []

    def together(ref):
        sent.append(ref)
        return len(sent) - 1

    def send(src, dst, group=None, **to):
        i = together(dst) if group is None else group
        pltpu.make_async_remote_copy(src, dst, send_sem.at[i], recv_sem.at[i],
                                     device_id=device(**to), device_id_type=MESH).start()
        return i

    def got(*groups):
        for i in groups:
            pltpu.make_async_copy(sent[i], sent[i], recv_sem.at[i]).wait()

    def left(*groups):
        for i in groups:
            pltpu.make_async_copy(sent[i], sent[i], send_sem.at[i]).wait()

    def dequantized(half, chunk, group):
        start = pl.multiple_of(half * HALF + chunk * 128, 128)
        turned = scales_v[:, pl.ds(start, 128)].T
        for block in range(group[0] // BLOCK, (group[0] + group[1]) // BLOCK):
            cols = slice(block * BLOCK, (block + 1) * BLOCK)
            yield cols, codes_v[pl.ds(start, 128), cols].astype(jnp.float32) * turned[:, block:block + 1]

    groups = (C, (0, AB))
    loads[0].wait()
    loads[1].wait()
    halves = []
    for group in groups:
        for chunk in range(2):
            rows = slice(chunk * 128, (chunk + 1) * 128)
            for cols, terms in dequantized(other, chunk, group):
                sib_out[rows, cols] = terms.astype(jnp.bfloat16)
        if group is C:
            pl.semaphore_wait(barrier, len(partners))
        cols = pl.ds(*group)
        halves.append(send(sib_out.at[:, cols], sib_in.at[:, cols], dc=1))

    first_step, second_step = {}, {}
    for group, half in zip(groups, halves):
        got(half)
        for chunk in range(2):
            rows = slice(chunk * 128, (chunk + 1) * 128)
            for cols, terms in dequantized(c, chunk, group):
                total = terms + sib_in[rows, cols].astype(jnp.float32)
                chip_sum[2 * chunk:2 * chunk + 2, :, :, cols] = total.astype(jnp.bfloat16).reshape(2, NX, PIECE, BLOCK)
        first_step[group] = together(line_in.at[:, :, :, pl.ds(*group)])
        along_x, along_y = (pl.ds(*cols) for cols in SPLIT[group])
        for i, d in enumerate(LINE):
            send(chip_sum.at[:, lax.rem(x + d + NX, NX), :, along_x], line_in.at[i, :, :, along_x], first_step[group], dx=d)
            send(chip_sum.at[lax.rem(y + d + NY, NY), :, :, along_y], line_in.at[i, :, :, along_y], first_step[group], dy=d)

    start = pl.multiple_of(c * HALF + y * 64 + x * PIECE, PIECE)

    def sum_line(group):
        got(first_step[group])
        for (low, width), own in zip(SPLIT[group], (chip_sum.at[:, x], chip_sum.at[y])):
            cols = slice(low, low + width)
            total = own[:, :, cols].astype(jnp.float32)
            for i in range(len(LINE)):
                total = total + line_in[i, :, :, cols].astype(jnp.float32)
            line_sum[:, :, cols] = total.astype(jnp.bfloat16)
        second_step[group] = together(last_in.at[:, :, pl.ds(*group)])
        along_x, along_y = (pl.ds(*cols) for cols in SPLIT[group])
        for i, d in enumerate(LINE):
            send(line_sum.at[lax.rem(y + d + NY, NY), :, along_x], last_in.at[i, :, along_x], second_step[group], dy=d)
            send(line_sum.at[lax.rem(x + d + NX, NX), :, along_y], last_in.at[i, :, along_y], second_step[group], dx=d)

    def summed(group):
        got(second_step[group])
        for (low, width), own in zip(SPLIT[group], (y, x)):
            cols = slice(low, low + width)
            total = line_sum[own, :, cols].astype(jnp.float32)
            for i in range(len(LINE)):
                total = total + last_in[i, :, cols].astype(jnp.float32)
            full[0, c, y, x, :, cols] = (total / 32).astype(jnp.bfloat16)
        return full[0, c, y, x, :, group[0]:group[0] + group[1]]

    def columns(wave, group):
        width = WAVES[wave][2]
        return pl.ds(0, width) if group == "A" else pl.ds(width, AB - width)

    def at(wave, rows_y, rows_x, group):
        first, count, _ = WAVES[wave]
        return full.at[pl.ds(first, count), c, rows_y, rows_x, :, columns(wave, group)]

    def second(wave, group):
        block = at(wave, y, x, group)
        three = together(at(wave, y, pl.ds(0, 3), group))
        for d in (1, -1, 2):
            send(block, block, three, **{"dx" if group == "A" else "dy": d})
        return three

    def brought(wave, group, back, rows=pl.ds(0, 4)):
        if group == "A":
            return at(wave, lax.rem(y - back + NY, NY), rows, group)
        return at(wave, rows, lax.rem(x - back + NX, NX), group)

    def third(wave, group):
        axis = "dy" if group == "A" else "dx"
        own = brought(wave, group, 0)
        return send(own, own, **{axis: 1}), send(own, own, **{axis: -1})

    def onward(wave, group, copies):
        axis = "dy" if group == "A" else "dx"
        going = []
        for i, (copy, step) in enumerate(zip(copies, (1, -1))):
            half = brought(wave, group, step, pl.ds(2 * i, 2))
            got(copy)
            going.append(send(half, half, **{axis: step}))
        return going

    def to_sibling(block):
        return send(block, block, dc=1)

    S2, S3, S4, handed = {}, {}, {}, []

    along = {}
    plane_c = together(sib_in.at[pl.ds(0, len(PLANE) * PIECE), pl.ds(*C)])

    def sum_c():
        summed(C)
        block = full.at[0, c, y, x, :, pl.ds(*C)]
        for dx, dy in PLANE:
            send(block, block, plane_c, dx=dx, dy=dy)

    def sum_ab():
        loads[2].wait()
        loads[3].wait()
        delta = summed(groups[1])
        piece[...] = step_of(delta, params_v[pl.ds(start, PIECE), :AB], momentum_v[pl.ds(start, PIECE), :AB])[0]
        for first, count, _ in WAVES[1:]:
            along[first] = together(full.at[pl.ds(first, count), c, y, x, :, pl.ds(0, AB)])
            for place in range(first, first + count):
                send(piece, full.at[place, c, y, x, :, pl.ds(0, AB)], along[first], dz=-NEAR[place])
        for group in GROUPS:
            S2[0, group] = second(0, group)

    def start_second(wave):
        got(along[WAVES[wave][0]])
        for group in GROUPS:
            S2[wave, group] = second(wave, group)

    def start_third(wave):
        for group in GROUPS:
            got(S2[wave, group])
            S3[wave, group] = third(wave, group)

    def start_onward(wave):
        for group in GROUPS:
            S4[wave, group] = onward(wave, group, S3[wave, group])

    own_parts = []

    def finish(wave):
        for group in GROUPS:
            got(*S4[wave, group])
            (handed if wave else own_parts).append(to_sibling(at(wave, slice(None), slice(None), group)))

    def ring_at(d, part):
        return full.at[PLACE[d], c, pl.ds(2 * part, 2), :, :, pl.ds(*C)]

    up, down = {}, {}

    def ring_start():
        got(plane_c)
        for row in range(NY):
            first = pl.multiple_of(c * HALF + row * 64, 64)
            cols = slice(C[0], C[0] + C[1])
            moved = full[0, c, row, :, :, cols].reshape(64, C[1])
            ring[row] = step_of(moved, params_v[pl.ds(first, 64), cols], momentum_v[pl.ds(first, 64), cols])[0].reshape(
                NX, PIECE, C[1])
            if row % 2:
                part = row // 2
                own = ring.at[pl.ds(2 * part, 2)]
                up[1, part] = send(own, ring_at(-1, part), dz=1)
                down[1, part] = send(own, ring_at(1, part), dz=-1)
        own_parts.append(to_sibling(full.at[0, c, :, :, :, pl.ds(*C)]))

    def ring_step(n):
        for part in range(2):
            if n < 4 or part == 0:
                got(up[n, part])
            if n < 4 or part == 1:
                got(down[n, part])
            if n < 3 or (n == 3 and part == 0):
                up[n + 1, part] = send(ring_at(-n, part), ring_at(-n - 1, part), dz=1)
            if n < 3 or (n == 3 and part == 1):
                down[n + 1, part] = send(ring_at(n, part), ring_at(n + 1, part), dz=-1)
        handed.append(to_sibling(full.at[pl.ds(PLACE[n], 2 if n < 4 else 1), c, :, :, :, pl.ds(*C)]))

    def own_rows():
        got(*own_parts)
        for i in range(2):
            for row in range(NY):
                first = i * HALF + row * 64
                moved = full[0, i, row].reshape(64, COLS)
                updated, moment = step_of(moved, params_v[first:first + 64], momentum_v[first:first + 64])
                own_params[first:first + 64] = updated
                own_moment[first:first + 64] = moment

    for act, *which in ORDER:
        {"line_c": lambda: sum_line(C), "line_ab": lambda: sum_line(groups[1]), "sum_c": sum_c, "sum_ab": sum_ab, "second": start_second, "third": start_third, "onward": start_onward,
         "finish": finish, "ring": ring_step, "ring_start": ring_start, "own": own_rows}[act](*which)
    left(*(i for i in range(len(sent)) if i not in handed))
    got(*handed)
    left(*handed)


def write_out(full, own_params, own_moment, new_params, new_momentum, sem):
    z = lax.axis_index("fsdp")
    copies = []
    for i, d in enumerate(NEAR[1:], 1):
        copies.append(pltpu.make_async_copy(full.at[i], new_params.at[lax.rem(z + d + NZ, NZ)], sem.at[i]))
    copies.append(pltpu.make_async_copy(own_params, new_params.at[z], sem.at[0]))
    copies.append(pltpu.make_async_copy(own_moment, new_momentum, sem.at[8]))
    for copy in copies:
        copy.start()
    for copy in copies:
        copy.wait()


def local(codes, block_scales, params, momentum):
    bf16 = jnp.bfloat16
    slab = (2, NY, NX, PIECE, COLS)
    hbm, vmem = pl.BlockSpec(memory_space=pltpu.HBM), pl.BlockSpec(memory_space=pltpu.VMEM)
    full, own_params, own_moment = pl.pallas_call(
        exchange,
        name="exchange",
        out_shape=(pltpu.VMEM((NZ, *slab), bf16), pltpu.VMEM((ROWS, COLS), bf16), pltpu.VMEM((ROWS, COLS), bf16)),
        in_specs=[hbm] * 4,
        out_specs=[vmem] * 3,
        scratch_shapes=[
            pltpu.VMEM((ROWS, COLS), bf16),
            pltpu.VMEM((COLS // BLOCK, ROWS), jnp.float32),
            pltpu.VMEM((ROWS, COLS), bf16),
            pltpu.VMEM((ROWS, COLS), bf16),
            pltpu.VMEM((HALF, COLS), bf16),
            pltpu.VMEM((HALF, COLS), bf16),
            pltpu.VMEM((NY, NX, PIECE, COLS), bf16),
            pltpu.VMEM((len(LINE), NY, PIECE, COLS), bf16),
            pltpu.VMEM((NY, PIECE, COLS), bf16),
            pltpu.VMEM((len(LINE), PIECE, COLS), bf16),
            pltpu.VMEM((PIECE, AB), bf16),
            pltpu.VMEM((NY, NX, PIECE, C[1]), bf16),
            pltpu.SemaphoreType.DMA((4,)),
            pltpu.SemaphoreType.DMA((COPIES,)),
            pltpu.SemaphoreType.DMA((COPIES,)),
        ],
        compiler_params=pltpu.CompilerParams(
            collective_id=0, has_side_effects=True, vmem_limit_bytes=50 * 2**20
        ),
    )(codes[0], block_scales[0].T, params, momentum)
    new_params, new_momentum = pl.pallas_call(
        write_out,
        name="write_out",
        out_shape=(jax.ShapeDtypeStruct((NZ, *slab), bf16), jax.ShapeDtypeStruct((ROWS, COLS), bf16)),
        in_specs=[vmem] * 3,
        out_specs=[hbm] * 2,
        scratch_shapes=[pltpu.SemaphoreType.DMA((9,))],
        compiler_params=pltpu.CompilerParams(vmem_limit_bytes=32 * 2**20),
    )(full, own_params.reshape(slab), own_moment)
    return new_params.reshape(NZ * ROWS, COLS), new_momentum


def solution(mesh):
    return jax.shard_map(
        local, mesh=mesh, in_specs=(P("rep", "fsdp", None), P("rep", "fsdp", None), P("fsdp", None), P("fsdp", None)),
        out_specs=(P(), P("fsdp", None)), check_vma=False
    )
```

```python
import functools

import jax
import jax.numpy as jnp
from jax import lax
from jax.experimental import pallas as pl
from jax.experimental.pallas import tpu as pltpu
from jax.sharding import PartitionSpec as P

MESH = pl.DeviceIdType.MESH
NX, NY, NZ = 4, 4, 8
ROWS, COLS, BLOCK = 512, 1024, 128
HALF = ROWS // 2
PIECE = 16
NEAR = (0, 1, -1, 2, -2, 3, -3, 4)
PLACE = {d: i for i, d in enumerate(NEAR)} | {-4: 7}
AB = 640
C = (AB, COLS - AB)
WAVES = ((0, 1, 384), (1, 2, 256), (3, 2, 256), (5, 3, 384))
SPLIT = {C: ((640, 128), (768, 256)), (0, AB): ((0, 384), (384, 256))}
LINE = (1, -1, 2)
PLANE = [(dx, dy) for dy in (0, 1, -1, 2) for dx in (0, 1, -1, 2) if (dx, dy) != (0, 0)]
GROUPS = ("A", "B")
COPIES = 160
ORDER = (("line_c",), ("line_ab",), ("sum_c",), ("sum_ab",), ("second", 1), ("ring_start",), ("second", 2), ("third", 0), ("second", 3), ("third", 1), ("ring", 1), ("third", 2), ("onward", 0), ("third", 3), ("onward", 1), ("ring", 2), ("finish", 0), ("onward", 2), ("onward", 3), ("finish", 1), ("ring", 3), ("finish", 2), ("finish", 3), ("own",), ("ring", 4))


def position():
    r, z = lax.axis_index("rep"), lax.axis_index("fsdp")
    return lax.rem(lax.div(r, 2), NX), lax.div(r, 2 * NX), z, lax.rem(r, 2)


def step_of(delta, params, momentum):
    delta = delta.astype(jnp.float32)
    moment = 0.9 * momentum.astype(jnp.float32) + delta
    updated = params.astype(jnp.float32) - 0.7 * (delta + 0.9 * moment)
    return updated.astype(jnp.bfloat16), moment.astype(jnp.bfloat16)


def exchange(codes, scales, params, momentum, full, own_params, own_moment,
             codes_v, scales_v, params_v, momentum_v, sib_out, sib_in, chip_sum, line_in, line_sum, last_in, piece, ring,
             load_sem, send_sem, recv_sem):
    x, y, z, c = position()
    other = 1 - c

    known = {}

    def device(dx=0, dy=0, dz=0, dc=0):
        to = (dx % NX, dy % NY, dz % NZ, dc)
        if to not in known:
            across = lax.rem(x + to[0], NX) if to[0] else x
            along_y = lax.rem(y + to[1], NY) if to[1] else y
            known[to] = (along_y * NX + across) * 2 + (other if dc else c), lax.rem(z + to[2], NZ) if to[2] else z
        return known[to]

    loads = [pltpu.make_async_copy(src, dst, load_sem.at[i]) for i, (src, dst) in enumerate(
        ((codes, codes_v), (scales, scales_v), (params, params_v), (momentum, momentum_v)))]
    for load in loads[:2]:
        load.start()

    barrier = pltpu.get_barrier_semaphore()
    partners = [dict(dc=1)] + [dict(dx=dx, dy=dy) for dx, dy in PLANE] + [dict(dz=dz) for dz in NEAR[1:]]
    for partner in partners:
        pl.semaphore_signal(barrier, inc=1, device_id=device(**partner), device_id_type=MESH)

    sent = []

    def together(ref):
        sent.append(ref)
        return len(sent) - 1

    def send(src, dst, group=None, **to):
        i = together(dst) if group is None else group
        pltpu.make_async_remote_copy(src, dst, send_sem.at[i], recv_sem.at[i],
                                     device_id=device(**to), device_id_type=MESH).start()
        return i

    def got(*groups):
        for i in groups:
            pltpu.make_async_copy(sent[i], sent[i], recv_sem.at[i]).wait()

    def left(*groups):
        for i in groups:
            pltpu.make_async_copy(sent[i], sent[i], send_sem.at[i]).wait()

    def dequantized(half, chunk, group):
        start = pl.multiple_of(half * HALF + chunk * 128, 128)
        turned = scales_v[:, pl.ds(start, 128)].T
        for block in range(group[0] // BLOCK, (group[0] + group[1]) // BLOCK):
            cols = slice(block * BLOCK, (block + 1) * BLOCK)
            yield cols, codes_v[pl.ds(start, 128), cols].astype(jnp.float32) * turned[:, block:block + 1]

    groups = (C, (0, AB))
    loads[0].wait()
    loads[1].wait()
    for load in loads[2:]:
        load.start()
    halves = []
    for group in groups:
        @pl.loop(0, 2)
        def _(chunk):
            rows = pl.ds(pl.multiple_of(chunk * 128, 128), 128)
            for cols, terms in dequantized(other, chunk, group):
                sib_out[rows, cols] = terms.astype(jnp.bfloat16)

        if group is C:
            pl.semaphore_wait(barrier, len(partners))
        cols = pl.ds(*group)
        halves.append(send(sib_out.at[:, cols], sib_in.at[:, cols], dc=1))

    first_step, second_step = {}, {}
    for group, half in zip(groups, halves):
        got(half)

        @pl.loop(0, 2)
        def _(chunk):
            rows = pl.ds(pl.multiple_of(chunk * 128, 128), 128)
            for cols, terms in dequantized(c, chunk, group):
                total = terms + sib_in[rows, cols].astype(jnp.float32)
                chip_sum[pl.ds(2 * chunk, 2), :, :, cols] = total.astype(jnp.bfloat16).reshape(2, NX, PIECE, BLOCK)

        first_step[group] = together(line_in.at[:, :, :, pl.ds(*group)])
        along_x, along_y = (pl.ds(*cols) for cols in SPLIT[group])
        for i, d in enumerate(LINE):
            send(chip_sum.at[:, lax.rem(x + d + NX, NX), :, along_x], line_in.at[i, :, :, along_x], first_step[group], dx=d)
            send(chip_sum.at[lax.rem(y + d + NY, NY), :, :, along_y], line_in.at[i, :, :, along_y], first_step[group], dy=d)

    start = pl.multiple_of(c * HALF + y * 64 + x * PIECE, PIECE)

    def sum_line(group):
        got(first_step[group])
        for (low, width), own in zip(SPLIT[group], (chip_sum.at[:, x], chip_sum.at[y])):
            cols = slice(low, low + width)
            total = own[:, :, cols].astype(jnp.float32)
            for i in range(len(LINE)):
                total = total + line_in[i, :, :, cols].astype(jnp.float32)
            line_sum[:, :, cols] = total.astype(jnp.bfloat16)
        second_step[group] = together(last_in.at[:, :, pl.ds(*group)])
        along_x, along_y = (pl.ds(*cols) for cols in SPLIT[group])
        for i, d in enumerate(LINE):
            send(line_sum.at[lax.rem(y + d + NY, NY), :, along_x], last_in.at[i, :, along_x], second_step[group], dy=d)
            send(line_sum.at[lax.rem(x + d + NX, NX), :, along_y], last_in.at[i, :, along_y], second_step[group], dx=d)

    def summed(group):
        got(second_step[group])
        for (low, width), own in zip(SPLIT[group], (y, x)):
            cols = slice(low, low + width)
            total = line_sum[own, :, cols].astype(jnp.float32)
            for i in range(len(LINE)):
                total = total + last_in[i, :, cols].astype(jnp.float32)
            full[0, c, y, x, :, cols] = (total / 32).astype(jnp.bfloat16)
        return full[0, c, y, x, :, group[0]:group[0] + group[1]]

    def columns(wave, group):
        width = WAVES[wave][2]
        return pl.ds(0, width) if group == "A" else pl.ds(width, AB - width)

    def at(wave, rows_y, rows_x, group):
        first, count, _ = WAVES[wave]
        return full.at[pl.ds(first, count), c, rows_y, rows_x, :, columns(wave, group)]

    def second(wave, group):
        block = at(wave, y, x, group)
        three = together(at(wave, y, pl.ds(0, 3), group))
        for d in (1, -1, 2):
            send(block, block, three, **{"dx" if group == "A" else "dy": d})
        return three

    def brought(wave, group, back, rows=pl.ds(0, 4)):
        if group == "A":
            return at(wave, lax.rem(y - back + NY, NY), rows, group)
        return at(wave, rows, lax.rem(x - back + NX, NX), group)

    def third(wave, group):
        axis = "dy" if group == "A" else "dx"
        own = brought(wave, group, 0)
        return send(own, own, **{axis: 1}), send(own, own, **{axis: -1})

    def onward(wave, group, copies):
        axis = "dy" if group == "A" else "dx"
        going = []
        for i, (copy, step) in enumerate(zip(copies, (1, -1))):
            half = brought(wave, group, step, pl.ds(2 * i, 2))
            got(copy)
            going.append(send(half, half, **{axis: step}))
        return going

    def to_sibling(block):
        return send(block, block, dc=1)

    S2, S3, S4, handed = {}, {}, {}, []

    along = {}
    plane_c = together(sib_in.at[pl.ds(0, len(PLANE) * PIECE), pl.ds(*C)])

    def sum_c():
        summed(C)
        block = full.at[0, c, y, x, :, pl.ds(*C)]
        for dx, dy in PLANE:
            send(block, block, plane_c, dx=dx, dy=dy)

    def sum_ab():
        loads[2].wait()
        loads[3].wait()
        delta = summed(groups[1])
        piece[...] = step_of(delta, params_v[pl.ds(start, PIECE), :AB], momentum_v[pl.ds(start, PIECE), :AB])[0]
        for first, count, _ in WAVES[1:]:
            along[first] = together(full.at[pl.ds(first, count), c, y, x, :, pl.ds(0, AB)])
            for place in range(first, first + count):
                send(piece, full.at[place, c, y, x, :, pl.ds(0, AB)], along[first], dz=-NEAR[place])
        for group in GROUPS:
            S2[0, group] = second(0, group)

    def start_second(wave):
        got(along[WAVES[wave][0]])
        for group in GROUPS:
            S2[wave, group] = second(wave, group)

    def start_third(wave):
        for group in GROUPS:
            got(S2[wave, group])
            S3[wave, group] = third(wave, group)

    def start_onward(wave):
        for group in GROUPS:
            S4[wave, group] = onward(wave, group, S3[wave, group])

    own_parts = []

    def finish(wave):
        for group in GROUPS:
            got(*S4[wave, group])
            (handed if wave else own_parts).append(to_sibling(at(wave, slice(None), slice(None), group)))

    def ring_at(d, part):
        return full.at[PLACE[d], c, part, :, :, pl.ds(*C)]

    up, down = {}, {}

    def ring_start():
        got(plane_c)
        cols = slice(C[0], C[0] + C[1])

        @pl.loop(0, NY)
        def _(row):
            first = pl.multiple_of(c * HALF + row * 64, 64)
            moved = full[0, c, row, :, :, cols].reshape(64, C[1])
            ring[row] = step_of(moved, params_v[pl.ds(first, 64), cols], momentum_v[pl.ds(first, 64), cols])[0].reshape(
                NX, PIECE, C[1])

        for part in range(NY):
            up[1, part] = send(ring.at[part], ring_at(-1, part), dz=1)
            down[1, part] = send(ring.at[part], ring_at(1, part), dz=-1)
        own_parts.append(to_sibling(full.at[0, c, :, :, :, pl.ds(*C)]))

    def ring_step(n):
        for part in range(NY):
            if n < 4 or part < 2:
                got(up[n, part])
            if n < 4 or part >= 2:
                got(down[n, part])
            if n < 3 or (n == 3 and part < 2):
                up[n + 1, part] = send(ring_at(-n, part), ring_at(-n - 1, part), dz=1)
            if n < 3 or (n == 3 and part >= 2):
                down[n + 1, part] = send(ring_at(n, part), ring_at(n + 1, part), dz=-1)
        handed.append(to_sibling(full.at[pl.ds(PLACE[n], 2 if n < 4 else 1), c, :, :, :, pl.ds(*C)]))

    def own_rows():
        got(*own_parts)
        @pl.loop(0, 2 * NY)
        def _(row):
            rows = pl.ds(pl.multiple_of(row * 64, 64), 64)
            moved = full[0, lax.div(row, NY), lax.rem(row, NY)].reshape(64, COLS)
            own_params[rows], own_moment[rows] = step_of(moved, params_v[rows], momentum_v[rows])

    for act, *which in ORDER:
        {"line_c": lambda: sum_line(C), "line_ab": lambda: sum_line(groups[1]), "sum_c": sum_c, "sum_ab": sum_ab, "second": start_second, "third": start_third, "onward": start_onward,
         "finish": finish, "ring": ring_step, "ring_start": ring_start, "own": own_rows}[act](*which)
    left(*(i for i in range(len(sent)) if i not in handed))
    got(*handed)
    left(*handed)


def write_out(full, own_params, own_moment, new_params, new_momentum, sem):
    z = lax.axis_index("fsdp")
    copies = []
    for i, d in enumerate(NEAR[1:], 1):
        copies.append(pltpu.make_async_copy(full.at[i], new_params.at[lax.rem(z + d + NZ, NZ)], sem.at[i]))
    copies.append(pltpu.make_async_copy(own_params, new_params.at[z], sem.at[0]))
    copies.append(pltpu.make_async_copy(own_moment, new_momentum, sem.at[8]))
    for copy in copies:
        copy.start()
    for copy in copies:
        copy.wait()


def local(codes, block_scales, params, momentum):
    bf16 = jnp.bfloat16
    slab = (2, NY, NX, PIECE, COLS)
    hbm, vmem = pl.BlockSpec(memory_space=pltpu.HBM), pl.BlockSpec(memory_space=pltpu.VMEM)
    full, own_params, own_moment = pl.pallas_call(
        exchange,
        name="exchange",
        out_shape=(pltpu.VMEM((NZ, *slab), bf16), pltpu.VMEM((ROWS, COLS), bf16), pltpu.VMEM((ROWS, COLS), bf16)),
        in_specs=[hbm] * 4,
        out_specs=[vmem] * 3,
        scratch_shapes=[
            pltpu.VMEM((ROWS, COLS), bf16),
            pltpu.VMEM((COLS // BLOCK, ROWS), jnp.float32),
            pltpu.VMEM((ROWS, COLS), bf16),
            pltpu.VMEM((ROWS, COLS), bf16),
            pltpu.VMEM((HALF, COLS), bf16),
            pltpu.VMEM((HALF, COLS), bf16),
            pltpu.VMEM((NY, NX, PIECE, COLS), bf16),
            pltpu.VMEM((len(LINE), NY, PIECE, COLS), bf16),
            pltpu.VMEM((NY, PIECE, COLS), bf16),
            pltpu.VMEM((len(LINE), PIECE, COLS), bf16),
            pltpu.VMEM((PIECE, AB), bf16),
            pltpu.VMEM((NY, NX, PIECE, C[1]), bf16),
            pltpu.SemaphoreType.DMA((4,)),
            pltpu.SemaphoreType.DMA((COPIES,)),
            pltpu.SemaphoreType.DMA((COPIES,)),
        ],
        compiler_params=pltpu.CompilerParams(
            collective_id=0, has_side_effects=True, vmem_limit_bytes=50 * 2**20
        ),
    )(codes[0], block_scales[0].T, params, momentum)
    new_params, new_momentum = pl.pallas_call(
        write_out,
        name="write_out",
        out_shape=(jax.ShapeDtypeStruct((NZ, *slab), bf16), jax.ShapeDtypeStruct((ROWS, COLS), bf16)),
        in_specs=[vmem] * 3,
        out_specs=[hbm] * 2,
        scratch_shapes=[pltpu.SemaphoreType.DMA((9,))],
        compiler_params=pltpu.CompilerParams(vmem_limit_bytes=32 * 2**20),
    )(full, own_params.reshape(slab), own_moment)
    return new_params.reshape(NZ * ROWS, COLS), new_momentum


def solution(mesh):
    return jax.shard_map(
        local, mesh=mesh, in_specs=(P("rep", "fsdp", None), P("rep", "fsdp", None), P("fsdp", None), P("fsdp", None)),
        out_specs=(P(), P("fsdp", None)), check_vma=False
    )
```

```python
import functools

import jax
import jax.numpy as jnp
from jax import lax
from jax.experimental import pallas as pl
from jax.experimental.pallas import tpu as pltpu
from jax.sharding import PartitionSpec as P

MESH = pl.DeviceIdType.MESH
NX, NY, NZ = 4, 4, 8
ROWS, COLS, BLOCK = 512, 1024, 128
HALF = ROWS // 2
PIECE = 16
NEAR = (0, 1, -1, 2, -2, 3, -3, 4)
PLACE = {d: i for i, d in enumerate(NEAR)} | {-4: 7}
AB = 640
C = (AB, COLS - AB)
WAVES = ((0, 1, 384), (1, 2, 256), (3, 2, 256), (5, 3, 384))
SPLIT = {C: ((640, 128), (768, 256)), (0, AB): ((0, 384), (384, 256))}
LINE = (1, -1, 2)
PLANE = [(dx, dy) for dy in (0, 1, -1, 2) for dx in (0, 1, -1, 2) if (dx, dy) != (0, 0)]
GROUPS = ("A", "B")
COPIES = 160
ORDER = (("line_c",), ("line_ab",), ("sum_c",), ("sum_ab",), ("second", 1), ("ring_start",), ("second", 2), ("third", 0), ("second", 3), ("third", 1), ("ring", 1, 0, 2), ("third", 2), ("ring", 1, 2, 4), ("onward", 0), ("third", 3), ("onward", 1), ("ring", 2, 0, 2), ("finish", 0), ("onward", 2), ("ring", 2, 2, 4), ("onward", 3), ("finish", 1), ("ring", 3, 0, 2), ("finish", 2), ("ring", 3, 2, 4), ("finish", 3), ("own",), ("ring", 4))


def position():
    r, z = lax.axis_index("rep"), lax.axis_index("fsdp")
    return lax.rem(lax.div(r, 2), NX), lax.div(r, 2 * NX), z, lax.rem(r, 2)


def step_of(delta, params, momentum):
    delta = delta.astype(jnp.float32)
    moment = 0.9 * momentum.astype(jnp.float32) + delta
    updated = params.astype(jnp.float32) - 0.7 * (delta + 0.9 * moment)
    return updated.astype(jnp.bfloat16), moment.astype(jnp.bfloat16)


def exchange(codes, scales, params, momentum, full, own_params, own_moment,
             codes_v, scales_v, params_v, momentum_v, sib_out, sib_in, chip_sum, line_in, line_sum, last_in, piece, ring,
             load_sem, send_sem, recv_sem):
    x, y, z, c = position()
    other = 1 - c

    known = {}

    def device(dx=0, dy=0, dz=0, dc=0):
        to = (dx % NX, dy % NY, dz % NZ, dc)
        if to not in known:
            across = lax.rem(x + to[0], NX) if to[0] else x
            along_y = lax.rem(y + to[1], NY) if to[1] else y
            known[to] = (along_y * NX + across) * 2 + (other if dc else c), lax.rem(z + to[2], NZ) if to[2] else z
        return known[to]

    loads = [pltpu.make_async_copy(src, dst, load_sem.at[i]) for i, (src, dst) in enumerate(
        ((codes, codes_v), (scales, scales_v), (params, params_v), (momentum, momentum_v)))]
    for load in loads[:2]:
        load.start()

    barrier = pltpu.get_barrier_semaphore()
    partners = [dict(dc=1)] + [dict(dx=dx, dy=dy) for dx, dy in PLANE] + [dict(dz=dz) for dz in NEAR[1:]]
    for partner in partners:
        pl.semaphore_signal(barrier, inc=1, device_id=device(**partner), device_id_type=MESH)

    sent = []

    def together(ref):
        sent.append(ref)
        return len(sent) - 1

    def send(src, dst, group=None, **to):
        i = together(dst) if group is None else group
        pltpu.make_async_remote_copy(src, dst, send_sem.at[i], recv_sem.at[i],
                                     device_id=device(**to), device_id_type=MESH).start()
        return i

    def got(*groups):
        for i in groups:
            pltpu.make_async_copy(sent[i], sent[i], recv_sem.at[i]).wait()

    def left(*groups):
        for i in groups:
            pltpu.make_async_copy(sent[i], sent[i], send_sem.at[i]).wait()

    def dequantized(half, chunk, group):
        start = pl.multiple_of(half * HALF + chunk * 128, 128)
        turned = scales_v[:, pl.ds(start, 128)].T
        for block in range(group[0] // BLOCK, (group[0] + group[1]) // BLOCK):
            cols = slice(block * BLOCK, (block + 1) * BLOCK)
            yield cols, codes_v[pl.ds(start, 128), cols].astype(jnp.float32) * turned[:, block:block + 1]

    groups = (C, (0, AB))
    loads[0].wait()
    loads[1].wait()
    for load in loads[2:]:
        load.start()
    halves = []
    for group in groups:
        @pl.loop(0, 2)
        def _(chunk):
            rows = pl.ds(pl.multiple_of(chunk * 128, 128), 128)
            for cols, terms in dequantized(other, chunk, group):
                sib_out[rows, cols] = terms.astype(jnp.bfloat16)

        if group is C:
            pl.semaphore_wait(barrier, len(partners))
        cols = pl.ds(*group)
        halves.append(send(sib_out.at[:, cols], sib_in.at[:, cols], dc=1))

    first_step, second_step = {}, {}
    for group, half in zip(groups, halves):
        got(half)

        @pl.loop(0, 2)
        def _(chunk):
            rows = pl.ds(pl.multiple_of(chunk * 128, 128), 128)
            for cols, terms in dequantized(c, chunk, group):
                total = terms + sib_in[rows, cols].astype(jnp.float32)
                chip_sum[pl.ds(2 * chunk, 2), :, :, cols] = total.astype(jnp.bfloat16).reshape(2, NX, PIECE, BLOCK)

        first_step[group] = together(line_in.at[:, :, :, pl.ds(*group)])
        along_x, along_y = (pl.ds(*cols) for cols in SPLIT[group])
        for i, d in enumerate(LINE):
            send(chip_sum.at[:, lax.rem(x + d + NX, NX), :, along_x], line_in.at[i, :, :, along_x], first_step[group], dx=d)
            send(chip_sum.at[lax.rem(y + d + NY, NY), :, :, along_y], line_in.at[i, :, :, along_y], first_step[group], dy=d)

    start = pl.multiple_of(c * HALF + y * 64 + x * PIECE, PIECE)

    def sum_line(group):
        got(first_step[group])
        for (low, width), own in zip(SPLIT[group], (chip_sum.at[:, x], chip_sum.at[y])):
            cols = slice(low, low + width)
            total = own[:, :, cols].astype(jnp.float32)
            for i in range(len(LINE)):
                total = total + line_in[i, :, :, cols].astype(jnp.float32)
            line_sum[:, :, cols] = total.astype(jnp.bfloat16)
        second_step[group] = together(last_in.at[:, :, pl.ds(*group)])
        along_x, along_y = (pl.ds(*cols) for cols in SPLIT[group])
        for i, d in enumerate(LINE):
            send(line_sum.at[lax.rem(y + d + NY, NY), :, along_x], last_in.at[i, :, along_x], second_step[group], dy=d)
            send(line_sum.at[lax.rem(x + d + NX, NX), :, along_y], last_in.at[i, :, along_y], second_step[group], dx=d)

    def summed(group):
        got(second_step[group])
        for (low, width), own in zip(SPLIT[group], (y, x)):
            cols = slice(low, low + width)
            total = line_sum[own, :, cols].astype(jnp.float32)
            for i in range(len(LINE)):
                total = total + last_in[i, :, cols].astype(jnp.float32)
            full[0, c, y, x, :, cols] = (total / 32).astype(jnp.bfloat16)
        return full[0, c, y, x, :, group[0]:group[0] + group[1]]

    def columns(wave, group):
        width = WAVES[wave][2]
        return pl.ds(0, width) if group == "A" else pl.ds(width, AB - width)

    def at(wave, rows_y, rows_x, group):
        first, count, _ = WAVES[wave]
        return full.at[pl.ds(first, count), c, rows_y, rows_x, :, columns(wave, group)]

    def second(wave, group):
        block = at(wave, y, x, group)
        three = together(at(wave, y, pl.ds(0, 3), group))
        for d in (1, -1, 2):
            send(block, block, three, **{"dx" if group == "A" else "dy": d})
        return three

    def brought(wave, group, back, rows=pl.ds(0, 4)):
        if group == "A":
            return at(wave, lax.rem(y - back + NY, NY), rows, group)
        return at(wave, rows, lax.rem(x - back + NX, NX), group)

    def third(wave, group):
        axis = "dy" if group == "A" else "dx"
        own = brought(wave, group, 0)
        return send(own, own, **{axis: 1}), send(own, own, **{axis: -1})

    def onward(wave, group, copies):
        axis = "dy" if group == "A" else "dx"
        going = []
        for i, (copy, step) in enumerate(zip(copies, (1, -1))):
            half = brought(wave, group, step, pl.ds(2 * i, 2))
            got(copy)
            going.append(send(half, half, **{axis: step}))
        return going

    def to_sibling(block):
        return send(block, block, dc=1)

    S2, S3, S4, handed = {}, {}, {}, []

    along = {}
    plane_c = together(sib_in.at[pl.ds(0, len(PLANE) * PIECE), pl.ds(*C)])

    def sum_c():
        summed(C)
        block = full.at[0, c, y, x, :, pl.ds(*C)]
        for dx, dy in PLANE:
            send(block, block, plane_c, dx=dx, dy=dy)

    def sum_ab():
        loads[2].wait()
        loads[3].wait()
        delta = summed(groups[1])
        piece[...] = step_of(delta, params_v[pl.ds(start, PIECE), :AB], momentum_v[pl.ds(start, PIECE), :AB])[0]
        for first, count, _ in WAVES[1:]:
            along[first] = together(full.at[pl.ds(first, count), c, y, x, :, pl.ds(0, AB)])
            for place in range(first, first + count):
                send(piece, full.at[place, c, y, x, :, pl.ds(0, AB)], along[first], dz=-NEAR[place])
        for group in GROUPS:
            S2[0, group] = second(0, group)

    def start_second(wave):
        got(along[WAVES[wave][0]])
        for group in GROUPS:
            S2[wave, group] = second(wave, group)

    def start_third(wave):
        for group in GROUPS:
            got(S2[wave, group])
            S3[wave, group] = third(wave, group)

    def start_onward(wave):
        for group in GROUPS:
            S4[wave, group] = onward(wave, group, S3[wave, group])

    own_parts = []

    def finish(wave):
        for group in GROUPS:
            got(*S4[wave, group])
            (handed if wave else own_parts).append(to_sibling(at(wave, slice(None), slice(None), group)))

    def ring_at(d, part):
        return full.at[PLACE[d], c, part, :, :, pl.ds(*C)]

    up, down = {}, {}

    def ring_start():
        got(plane_c)
        cols = slice(C[0], C[0] + C[1])

        @pl.loop(0, NY)
        def _(row):
            first = pl.multiple_of(c * HALF + row * 64, 64)
            moved = full[0, c, row, :, :, cols].reshape(64, C[1])
            ring[row] = step_of(moved, params_v[pl.ds(first, 64), cols], momentum_v[pl.ds(first, 64), cols])[0].reshape(
                NX, PIECE, C[1])

        for part in range(NY):
            up[1, part] = send(ring.at[part], ring_at(-1, part), dz=1)
            down[1, part] = send(ring.at[part], ring_at(1, part), dz=-1)
        own_parts.append(to_sibling(full.at[0, c, :, :, :, pl.ds(*C)]))

    def ring_step(n, low=0, high=NY):
        for part in range(low, high):
            if n < 4 or part < 2:
                got(up[n, part])
            if n < 4 or part >= 2:
                got(down[n, part])
            if n < 3 or (n == 3 and part < 2):
                up[n + 1, part] = send(ring_at(-n, part), ring_at(-n - 1, part), dz=1)
            if n < 3 or (n == 3 and part >= 2):
                down[n + 1, part] = send(ring_at(n, part), ring_at(n + 1, part), dz=-1)
        if high == NY:
            handed.append(to_sibling(full.at[pl.ds(PLACE[n], 2 if n < 4 else 1), c, :, :, :, pl.ds(*C)]))

    def own_rows():
        got(*own_parts)
        @pl.loop(0, 2 * NY)
        def _(row):
            rows = pl.ds(pl.multiple_of(row * 64, 64), 64)
            moved = full[0, lax.div(row, NY), lax.rem(row, NY)].reshape(64, COLS)
            own_params[rows], own_moment[rows] = step_of(moved, params_v[rows], momentum_v[rows])

    for act, *which in ORDER:
        {"line_c": lambda: sum_line(C), "line_ab": lambda: sum_line(groups[1]), "sum_c": sum_c, "sum_ab": sum_ab, "second": start_second, "third": start_third, "onward": start_onward,
         "finish": finish, "ring": ring_step, "ring_start": ring_start, "own": own_rows}[act](*which)
    left(*(i for i in range(len(sent)) if i not in handed))
    got(*handed)
    left(*handed)


def write_out(full, own_params, own_moment, new_params, new_momentum, sem):
    z = lax.axis_index("fsdp")
    copies = []
    for i, d in enumerate(NEAR[1:], 1):
        copies.append(pltpu.make_async_copy(full.at[i], new_params.at[lax.rem(z + d + NZ, NZ)], sem.at[i]))
    copies.append(pltpu.make_async_copy(own_params, new_params.at[z], sem.at[0]))
    copies.append(pltpu.make_async_copy(own_moment, new_momentum, sem.at[8]))
    for copy in copies:
        copy.start()
    for copy in copies:
        copy.wait()


def local(codes, block_scales, params, momentum):
    bf16 = jnp.bfloat16
    slab = (2, NY, NX, PIECE, COLS)
    hbm, vmem = pl.BlockSpec(memory_space=pltpu.HBM), pl.BlockSpec(memory_space=pltpu.VMEM)
    full, own_params, own_moment = pl.pallas_call(
        exchange,
        name="exchange",
        out_shape=(pltpu.VMEM((NZ, *slab), bf16), pltpu.VMEM((ROWS, COLS), bf16), pltpu.VMEM((ROWS, COLS), bf16)),
        in_specs=[hbm] * 4,
        out_specs=[vmem] * 3,
        scratch_shapes=[
            pltpu.VMEM((ROWS, COLS), bf16),
            pltpu.VMEM((COLS // BLOCK, ROWS), jnp.float32),
            pltpu.VMEM((ROWS, COLS), bf16),
            pltpu.VMEM((ROWS, COLS), bf16),
            pltpu.VMEM((HALF, COLS), bf16),
            pltpu.VMEM((HALF, COLS), bf16),
            pltpu.VMEM((NY, NX, PIECE, COLS), bf16),
            pltpu.VMEM((len(LINE), NY, PIECE, COLS), bf16),
            pltpu.VMEM((NY, PIECE, COLS), bf16),
            pltpu.VMEM((len(LINE), PIECE, COLS), bf16),
            pltpu.VMEM((PIECE, AB), bf16),
            pltpu.VMEM((NY, NX, PIECE, C[1]), bf16),
            pltpu.SemaphoreType.DMA((4,)),
            pltpu.SemaphoreType.DMA((COPIES,)),
            pltpu.SemaphoreType.DMA((COPIES,)),
        ],
        compiler_params=pltpu.CompilerParams(
            collective_id=0, has_side_effects=True, vmem_limit_bytes=50 * 2**20
        ),
    )(codes[0], block_scales[0].T, params, momentum)
    new_params, new_momentum = pl.pallas_call(
        write_out,
        name="write_out",
        out_shape=(jax.ShapeDtypeStruct((NZ, *slab), bf16), jax.ShapeDtypeStruct((ROWS, COLS), bf16)),
        in_specs=[vmem] * 3,
        out_specs=[hbm] * 2,
        scratch_shapes=[pltpu.SemaphoreType.DMA((9,))],
        compiler_params=pltpu.CompilerParams(vmem_limit_bytes=32 * 2**20),
    )(full, own_params.reshape(slab), own_moment)
    return new_params.reshape(NZ * ROWS, COLS), new_momentum


def solution(mesh):
    return jax.shard_map(
        local, mesh=mesh, in_specs=(P("rep", "fsdp", None), P("rep", "fsdp", None), P("fsdp", None), P("fsdp", None)),
        out_specs=(P(), P("fsdp", None)), check_vma=False
    )
```
